32 devices in a mesh: lat: 16 (over z, x, core), lon: 2 (over y).
Axes of the slice: x: 2, y: 2, z: 4, core: 2. Of those that a mesh axis runs over, the one named last changes fastest.
Arguments:
- field: bfloat16 [768, 3600, 128], P('lat', 'lon'), may hold values from -6 to 6
- spectral_weight: bfloat16 [64, 2, 128, 128], P('lon'), may hold values from -0.375 to 0.375
- conv_weight: bfloat16 [3, 3, 128, 128], replicated, may hold values from -0.1875 to 0.1875
- conv_bias: float32 [128], replicated, may hold values from -3 to 3
Outputs:
- block_out: bfloat16 [768, 3600, 128], P('lat', 'lon')
The draws below stay inside these ranges and needn't reach their ends.
All inputs are finite; a program needn't handle non-finite values.
Results may differ from the reference program's by a relative error of at most 0.0052.
Values may be sent and summed in bfloat16 or wider, within the bound.
A program may use at most 832 MiB of HBM per device.

```python
import math
import jax
import jax.numpy as jnp
from jax import lax

C = 128
M = 64
NLON = 3600
LAT_DEV = 48
NLAT = 768
N_LAT = 16


def block_levels(rng, shape, cuts, least, top_value):
    gain, own = 1.0, jax.random.fold_in(rng, 6)
    for dim, blocks in cuts:
        heights = jnp.exp(jax.random.uniform(jax.random.fold_in(own, dim), (blocks,), jnp.float32, least / len(cuts), top_value / len(cuts)))
        gain = gain * jnp.repeat(heights, shape[dim] // blocks).reshape([-1 if axis == dim else 1 for axis in range(len(shape))])
    return gain


def centred(stream_key, dims, scale, most, split=(), kind=jnp.bfloat16):
    gain = block_levels(stream_key, dims, split, -0.22, 0.18) if split else 1.0
    values = jax.random.normal(stream_key, dims, jnp.float32) * scale * gain
    return jnp.minimum(jnp.maximum(values, -most), most).astype(kind)


def setup_inputs(seed: int = 0) -> dict:
    key_list = jax.random.split(jax.random.key(seed), 5)
    return {
        "field": centred(key_list[0], (NLAT, NLON, C), 1.0, 6.0, ((0, 16), (1, 2))),
        "spectral_weight": centred(key_list[1], (M, 2, C, C), (2 * C) ** -0.5, 0.375, ((0, 2),)),
        "conv_weight": centred(key_list[2], (3, 3, C, C), (9 * C) ** -0.5, 0.1875),
        "conv_bias": centred(key_list[3], (C,), 0.5, 3.0, (), jnp.float32),
    }


def forward_table(start, count, lon_start, lon_count):
    modes = (jnp.arange(count, dtype=jnp.int32) + start)[:, None]
    places = (jnp.arange(lon_count, dtype=jnp.int32) + lon_start)[None, :]
    phase_index = modes * places % NLON
    angle = phase_index.astype(jnp.float32) * (2.0 * math.pi / NLON)
    scale = 1.0 / math.sqrt(NLON)
    table = jnp.stack([jnp.cos(angle) * scale, -jnp.sin(angle) * scale], axis=1)
    return table.astype(jnp.bfloat16)

def inverse_table(start, count, lon_start, lon_count):
    modes = (jnp.arange(count, dtype=jnp.int32) + start)[:, None]
    places = (jnp.arange(lon_count, dtype=jnp.int32) + lon_start)[None, :]
    phase_index = modes * places % NLON
    angle = phase_index.astype(jnp.float32) * (2.0 * math.pi / NLON)
    weight = jnp.where(modes == 0, 1.0, 2.0).astype(jnp.float32) / math.sqrt(4.0 * M)
    table = jnp.stack([weight * jnp.cos(angle), -weight * jnp.sin(angle)], axis=1)
    return table.astype(jnp.bfloat16)

def reference(field, spectral_weight, conv_weight, conv_bias):
    wrapped = jnp.concatenate([field[:, -1:], field, field[:, :1]], axis=1)
    zero_row = jnp.zeros((1, NLON + 2, C), jnp.bfloat16)
    padded = jnp.concatenate([zero_row, wrapped, zero_row], axis=0)
    fwd_table = forward_table(0, M, 0, NLON).astype(jnp.float32)
    inv_table = inverse_table(0, M, 0, NLON).astype(jnp.float32)
    w_real = spectral_weight[:, 0].astype(jnp.float32)
    w_imag = spectral_weight[:, 1].astype(jnp.float32)
    kernel = conv_weight.astype(jnp.float32)

    def band(number):
        band_rows = lax.dynamic_slice_in_dim(padded, number * LAT_DEV, LAT_DEV + 2, 0)
        inner = band_rows[1:-1, 1:-1].astype(jnp.float32)
        spectrum = jnp.einsum('mrn,lnc->mrlc', fwd_table, inner)
        spec_b = spectrum.astype(jnp.bfloat16).astype(jnp.float32)
        part_real = jnp.einsum('mlc,mcd->mld', spec_b[:, 0], w_real) - jnp.einsum('mlc,mcd->mld', spec_b[:, 1], w_imag)
        part_imag = jnp.einsum('mlc,mcd->mld', spec_b[:, 0], w_imag) + jnp.einsum('mlc,mcd->mld', spec_b[:, 1], w_real)
        mixed = jnp.stack([part_real, part_imag], axis=1).astype(jnp.bfloat16).astype(jnp.float32)
        spectral = jnp.einsum('mrn,mrlc->lnc', inv_table, mixed)
        wide = band_rows.astype(jnp.float32)
        bypass = jnp.zeros((LAT_DEV, NLON, C), jnp.float32)
        for i in range(3):
            for j in range(3):
                bypass = bypass + jnp.einsum('lnc,cd->lnd', wide[i:i + LAT_DEV, j:j + NLON], kernel[i, j])
        return jax.nn.gelu(spectral + bypass + conv_bias).astype(jnp.bfloat16)
    bands = lax.map(band, jnp.arange(N_LAT, dtype=jnp.int32))
    return bands.reshape(NLAT, NLON, C)
```

```python
import functools
import math

import jax
import jax.numpy as jnp
import ml_dtypes
import numpy as np
from jax import lax
from jax.experimental import pallas as pl
from jax.experimental.pallas import tpu as pltpu
from jax.sharding import PartitionSpec as P

M = 64
NLON = 3600
TILE = 256
LAG = 16
VMEM = 56 * 1024 * 1024


def tables(shards, lon_dev, modes_local):
    angle = np.arange(NLON, dtype=np.float32) * np.float32(2.0 * math.pi / NLON)
    cos, sin = np.cos(angle), np.sin(angle)
    forward, inverse = [], []
    for index in range(shards):
        places = np.arange(lon_dev) + index * lon_dev

        def rows(step):
            owners = [(index + step * s) % shards for s in range(shards)]
            modes = np.concatenate([np.arange(modes_local) + o * modes_local for o in owners])
            return modes, modes[:, None] * places[None, :] % NLON

        modes, phase = rows(1)
        scale = np.float32(1.0 / math.sqrt(NLON))
        table = np.stack([cos[phase] * scale, -sin[phase] * scale], axis=1)
        forward.append(table.reshape(2 * len(modes), lon_dev))
        modes, phase = rows(-1)
        weight = (np.where(modes == 0, 1.0, 2.0) / math.sqrt(4.0 * M)).astype(np.float32)[:, None]
        table = np.stack([weight * cos[phase], -weight * sin[phase]], axis=1)
        inverse.append(table.reshape(2 * len(modes), lon_dev).T)
    return (
        np.stack(forward).astype(ml_dtypes.bfloat16),
        np.stack(inverse).astype(ml_dtypes.bfloat16),
    )


def dft_kernel(mine, index_ref, table_ref, x_ref, own_ref, send_ref):
    rows = x_ref.shape[0]
    channels = x_ref.shape[2]
    for l in range(0, rows, 2):
        pair = jnp.concatenate([x_ref[l], x_ref[l + 1]], axis=1)
        part = jnp.dot(table_ref[...], pair, preferred_element_type=jnp.float32)
        for d in range(2):
            half = part[:, d * channels : (d + 1) * channels]
            own_ref[l + d] = half[:mine]
            send_ref[l + d] = half[mine:].astype(jnp.bfloat16)


def forward_dft(index, field, table, mine):
    lat, lon, channels = field.shape
    rows = 8
    count = table.shape[1]
    return pl.pallas_call(
        functools.partial(dft_kernel, mine),
        grid_spec=pltpu.PrefetchScalarGridSpec(
            num_scalar_prefetch=1,
            grid=(lat // rows,),
            in_specs=[
                pl.BlockSpec((None, count, lon), lambda i, index: (index[0], 0, 0)),
                pl.BlockSpec((rows, lon, channels), lambda i, index: (i, 0, 0)),
            ],
            out_specs=[
                pl.BlockSpec((rows, mine, channels), lambda i, index: (i, 0, 0)),
                pl.BlockSpec((rows, count - mine, channels), lambda i, index: (i, 0, 0)),
            ],
        ),
        out_shape=[
            jax.ShapeDtypeStruct((lat, mine, channels), jnp.float32),
            jax.ShapeDtypeStruct((lat, count - mine, channels), jnp.bfloat16),
        ],
        compiler_params=pltpu.CompilerParams(vmem_limit_bytes=VMEM),
        cost_estimate=pl.CostEstimate(
            flops=2 * count * lat * lon * channels,
            bytes_accessed=2 * lat * lon * channels + 6 * lat * count * channels,
            transcendentals=0,
        ),
        name="forward_dft",
    )(index, table, field)


def mix_kernel(parts, own_ref, *refs):
    recv_refs, (w_ref, out_ref, s_ref, t_ref) = refs[:parts], refs[parts:]
    lat, mine, channels = own_ref.shape
    step = pl.program_id(0)
    group = w_ref.shape[0]

    @pl.when(step == 0)
    def _():
        total = own_ref[...]
        for recv_ref in recv_refs:
            total = total + recv_ref[...].astype(jnp.float32)
        s_ref[...] = total.reshape(lat * mine, channels)

    for g in range(group):
        m = step * group + g
        real = pl.ds(2 * m, lat, stride=mine)
        imag = pl.ds(2 * m + 1, lat, stride=mine)
        joined = jnp.concatenate(
            [s_ref[real, :].astype(jnp.bfloat16), s_ref[imag, :].astype(jnp.bfloat16)], axis=1
        )
        upper = jnp.concatenate([w_ref[g, 0], w_ref[g, 1]], axis=1)
        lower = jnp.concatenate([-w_ref[g, 1], w_ref[g, 0]], axis=1)
        block = jnp.concatenate([upper, lower], axis=0)
        product = jnp.dot(joined, block, preferred_element_type=jnp.float32)
        t_ref[real, :] = product[:, :channels]
        t_ref[imag, :] = product[:, channels:]

    @pl.when(step == pl.num_programs(0) - 1)
    def _():
        out_ref[...] = t_ref[...].reshape(lat, mine, channels).astype(jnp.bfloat16)


def mix_modes(own, received, spectral_weight):
    lat, mine, channels = own.shape
    modes = spectral_weight.shape[0]
    group = math.gcd(modes, 4)
    whole = pl.BlockSpec((lat, mine, channels), lambda i: (0, 0, 0))
    return pl.pallas_call(
        functools.partial(mix_kernel, len(received)),
        grid=(modes // group,),
        in_specs=[whole] * (1 + len(received))
        + [pl.BlockSpec((group, 2, channels, channels), lambda i: (i, 0, 0, 0))],
        out_specs=whole,
        out_shape=jax.ShapeDtypeStruct((lat, mine, channels), jnp.bfloat16),
        scratch_shapes=[pltpu.VMEM((lat * mine, channels), jnp.float32)] * 2,
        compiler_params=pltpu.CompilerParams(vmem_limit_bytes=VMEM),
        cost_estimate=pl.CostEstimate(
            flops=8 * modes * lat * channels * channels,
            bytes_accessed=4 * modes * channels * channels + 8 * lat * mine * channels,
            transcendentals=0,
        ),
        name="mix_modes",
    )(own, *received, spectral_weight)


def cuts(length):
    starts = list(range(0, max(length - TILE // 2, 1), TILE))
    return list(zip(starts, starts[1:] + [length]))


def convolve(a_ref, rows_ref, here, w_ref, low, high, channels, extra=None):
    lhs = jnp.concatenate([rows_ref[slot, low:high] for slot in here], axis=1)
    for j in range(3):
        result = jnp.dot(lhs, w_ref[j], preferred_element_type=jnp.float32)
        if j == 1 and extra is not None:
            result = result + jnp.dot(*extra, preferred_element_type=jnp.float32)
        for d in range(2):
            a_ref[j, d, 8 + low : 8 + high] = result[:, d * channels : (d + 1) * channels]


def taps(a_ref, d, low, size):
    return (
        a_ref[0, d, pl.ds(7 + low, size)]
        + a_ref[1, d, pl.ds(8 + low, size)]
        + a_ref[2, d, pl.ds(9 + low, size)]
    )


def stash_kernel(first, count, x_ref, w_ref, *refs):
    out_ref, rows_ref, a_ref, sems = refs[-4:]
    lon, channels = x_ref.shape[1:]
    step = pl.program_id(0)
    pair = first + step
    slots = rows_ref.shape[0]

    def fetch(place):
        slot = lax.rem(place, slots)
        return pltpu.make_async_copy(x_ref.at[place - 1], rows_ref.at[slot], sems.at[slot])

    @pl.when(step == 0)
    def _():
        for i in range(4):
            fetch(2 * pair + i).start()
        for i in range(2):
            fetch(2 * pair + i).wait()

    @pl.when(step + 1 < count)
    def _():
        for i in range(4, 6):
            fetch(2 * pair + i).start()

    for i in range(2, 4):
        fetch(2 * pair + i).wait()

    here = [lax.rem(2 * pair + i, slots) for i in range(4)]
    for d in range(2):
        a_ref[0, d, 7:8] = jnp.zeros((1, channels), jnp.float32)
        a_ref[2, d, 8 + lon : 9 + lon] = jnp.zeros((1, channels), jnp.float32)

    def finish(low, high):
        for d in range(2):
            out_ref[d, low:high] = taps(a_ref, d, low, high - low)

    done, ready = 0, 0
    for low, high in cuts(lon):
        convolve(a_ref, rows_ref, here, w_ref, low, high, channels)
        if ready > done:
            finish(done, ready)
            done = ready
        ready = high - LAG
    finish(done, lon)


def stash(field, weights, first, count, total, offset, before=None):
    lat, lon, channels = field.shape
    slots = 8
    extra = [] if before is None else [before]
    return pl.pallas_call(
        functools.partial(stash_kernel, first, count),
        grid=(count,),
        in_specs=[
            pl.BlockSpec(memory_space=pl.ANY),
            pl.BlockSpec(weights.shape, lambda i: (0, 0, 0)),
        ]
        + [pl.BlockSpec(memory_space=pl.ANY)] * len(extra),
        out_specs=pl.BlockSpec((2, lon, channels), lambda i: (i + offset, 0, 0)),
        out_shape=jax.ShapeDtypeStruct((2 * total, lon, channels), jnp.float32),
        input_output_aliases={2: 0} if extra else {},
        scratch_shapes=[
            pltpu.VMEM((slots, lon, channels), jnp.bfloat16),
            pltpu.VMEM((3, 2, (lon + 8) // 8 * 8 + 16, channels), jnp.float32),
            pltpu.SemaphoreType.DMA((slots,)),
        ],
        compiler_params=pltpu.CompilerParams(vmem_limit_bytes=VMEM),
        cost_estimate=pl.CostEstimate(
            flops=2 * 2 * count * lon * channels * 12 * channels,
            bytes_accessed=12 * count * lon * channels,
            transcendentals=0,
        ),
        name="stash",
    )(field, weights, *extra)


def block_kernel(
    stashed, pieces, index_ref, x_ref, halo_ref, stash_ref, w_ref, g_ref, edge_ref, bias_ref, *refs
):
    piece_refs, (out_ref, rows_ref, rhs_ref, a_ref, sems) = refs[:pieces], refs[pieces:]
    lat, lon, channels = x_ref.shape
    step = pl.program_id(0)
    slots = rows_ref.shape[0]
    last = lat // 2 - 1
    base = 1 + stashed
    wrap = lat + 2

    def virtual(at):
        return jnp.where(at == last, last + 2, at + 1)

    def fetch(source, place):
        slot = lax.rem(place, slots)
        return pltpu.make_async_copy(source, rows_ref.at[slot], sems.at[slot])

    def start(place):
        real = jnp.where(place >= wrap, place - wrap, place)

        @pl.when(real == 0)
        def _():
            fetch(halo_ref.at[0], place).start()

        @pl.when(real == lat + 1)
        def _():
            fetch(halo_ref.at[1], place).start()

        @pl.when(jnp.logical_and(real > 0, real < lat + 1))
        def _():
            fetch(x_ref.at[jnp.clip(real - 1, 0, lat - 1)], place).start()

    def wait(place):
        fetch(halo_ref.at[0], place).wait()

    def fresh(pair):
        return jnp.logical_or(pair == base, pair == last + 2)

    def begin(at):
        pair = virtual(at)

        @pl.when(fresh(pair))
        def _():
            start(2 * pair)
            start(2 * pair + 1)

        @pl.when(pair >= base)
        def _():
            start(2 * pair + 2)
            start(2 * pair + 3)

    if stashed == 0:
        @pl.when(step == 0)
        def _():
            begin(step)

    @pl.when(step < last)
    def _():
        begin(step + 1)

    top = 0
    for piece_ref in piece_refs:
        size = piece_ref.shape[1]
        for d in range(2):
            rhs_ref[top : top + size, d * channels : (d + 1) * channels] = piece_ref[d]
        top += size
    bias = bias_ref[...]
    c1 = math.sqrt(2.0 / math.pi)
    c2 = c1 * 0.044715

    def gelu(x):
        t = jnp.tanh(x * (c1 + c2 * (x * x)))
        return (x * (0.5 + 0.5 * t)).astype(jnp.bfloat16)

    pair = virtual(step)

    @pl.when(pair < base)
    def _():
        for low, high in cuts(lon):
            part = jnp.dot(g_ref[low:high], rhs_ref[...], preferred_element_type=jnp.float32)
            for d in range(2):
                x = part[:, d * channels : (d + 1) * channels] + stash_ref[d, low:high] + bias
                place = low + lax.broadcasted_iota(jnp.int32, x.shape, 0)
                if low == 0:
                    x = x + jnp.where(place == 0, edge_ref[d, 0:1], 0.0)
                if high == lon:
                    x = x + jnp.where(place == lon - 1, edge_ref[d, 1:2], 0.0)
                out_ref[d, low:high] = gelu(x)

    @pl.when(pair >= base)
    def _():
        @pl.when(fresh(pair))
        def _():
            wait(2 * pair)
            wait(2 * pair + 1)

        wait(2 * pair + 2)
        wait(2 * pair + 3)
        here = [lax.rem(2 * pair + i, slots) for i in range(4)]
        for d in range(2):
            a_ref[0, d, 7:8] = edge_ref[d, 0:1]
            a_ref[2, d, 8 + lon : 9 + lon] = edge_ref[d, 1:2]

        def finish(low, high):
            for d in range(2):
                out_ref[d, low:high] = gelu(taps(a_ref, d, low, high - low) + bias)

        done, ready = 0, 0
        for low, high in cuts(lon):
            extra = (g_ref[low:high], rhs_ref[...])
            convolve(a_ref, rows_ref, here, w_ref, low, high, channels, extra)
            if ready > done:
                finish(done, ready)
                done = ready
            ready = high - LAG
        finish(done, lon)


def block(index, field, halo, stashed, weights, table, edges, bias, pieces):
    lat, lon, channels = field.shape
    count = table.shape[2]
    slots = 8
    pairs = lat // 2
    held = stashed.shape[0] // 2

    def pair(i, index):
        return (lax.rem(i + 1, pairs), 0, 0)

    return pl.pallas_call(
        functools.partial(block_kernel, held, len(pieces)),
        grid_spec=pltpu.PrefetchScalarGridSpec(
            num_scalar_prefetch=1,
            grid=(pairs,),
            in_specs=[
                pl.BlockSpec(memory_space=pl.ANY),
                pl.BlockSpec(memory_space=pl.ANY),
                pl.BlockSpec(
                    (2, lon, channels), lambda i, index: (jnp.minimum(i, held - 1), 0, 0)
                ),
                pl.BlockSpec(weights.shape, lambda i, index: (0, 0, 0)),
                pl.BlockSpec((None, lon, count), lambda i, index: (index[0], 0, 0)),
                pl.BlockSpec((2, 2, channels), pair),
                pl.BlockSpec((1, channels), lambda i, index: (0, 0)),
            ]
            + [pl.BlockSpec((2, p.shape[1], channels), pair) for p in pieces],
            out_specs=pl.BlockSpec((2, lon, channels), pair),
            scratch_shapes=[
                pltpu.VMEM((slots, lon, channels), jnp.bfloat16),
                pltpu.VMEM((count, 2 * channels), jnp.bfloat16),
                pltpu.VMEM((3, 2, (lon + 8) // 8 * 8 + 16, channels), jnp.float32),
                pltpu.SemaphoreType.DMA((slots,)),
            ],
        ),
        out_shape=jax.ShapeDtypeStruct((lat, lon, channels), jnp.bfloat16),
        compiler_params=pltpu.CompilerParams(vmem_limit_bytes=VMEM),
        cost_estimate=pl.CostEstimate(
            flops=2 * lat * lon * channels * (9 * channels + count),
            bytes_accessed=4 * lat * lon * channels,
            transcendentals=lat * lon * channels,
        ),
        name="block",
    )(index, field, halo, stashed, weights, table, edges, bias, *pieces)


def shift(x, axis, by, periodic=True):
    count = lax.axis_size(axis)
    pairs = [(i, (i + by) % count) for i in range(count) if periodic or 0 <= i + by < count]
    return lax.ppermute(x, axis, pairs)


def pair_weights(conv_weight):
    zero = jnp.zeros_like(conv_weight[0, 0])
    return jnp.stack(
        [
            jnp.concatenate(
                [
                    jnp.concatenate([conv_weight[i, j] if i < 3 else zero for i in range(4)], axis=0),
                    jnp.concatenate([conv_weight[i - 1, j] if i else zero for i in range(4)], axis=0),
                ],
                axis=1,
            )
            for j in range(3)
        ]
    )


def per_device(field, spectral_weight, conv_weight, conv_bias):
    lat, lon, channels = field.shape
    modes_local = spectral_weight.shape[0]
    shards = lax.axis_size("lon")
    index = lax.axis_index("lon")
    mine = 2 * modes_local
    forward, inverse = tables(shards, lon, modes_local)
    index = index.astype(jnp.int32)[None]
    weights = pair_weights(conv_weight)

    own, send = forward_dft(index, field, jnp.asarray(forward), mine)
    received = [shift(send[:, (s - 1) * mine : s * mine], "lon", s) for s in range(1, shards)]

    outer = (field[lat - 1 :], field[:1], field[:, lon - 1], field[:, 0], weights)
    outer, send = lax.optimization_barrier((outer, send))
    low_row, high_row, east_column, west_column, weights = outer
    above = shift(low_row, "lat", 1, False)
    below = shift(high_row, "lat", -1, False)
    easts = jnp.concatenate([above[:, lon - 1], east_column, below[:, lon - 1]], axis=0)
    wests = jnp.concatenate([above[:, 0], west_column, below[:, 0]], axis=0)
    if shards == 2:
        columns = shift(jnp.stack([easts, wests], axis=1), "lon", 1)
    else:
        columns = jnp.stack([shift(easts, "lon", 1), shift(wests, "lon", -1)], axis=1)
    edges = jnp.stack(
        [
            sum(
                jnp.dot(
                    columns[i : i + lat, side],
                    conv_weight[i, 2 * side],
                    preferred_element_type=jnp.float32,
                )
                for i in range(3)
            )
            for side in range(2)
        ],
        axis=1,
    )
    halo = jnp.concatenate([above, below], axis=0)

    first, second = lat // 12, 7 * lat // 48
    total = first + second
    held = stash(field, weights, 1, first, total, 0)
    held, received = lax.optimization_barrier((held, received))
    mixed = mix_modes(own, received, spectral_weight)
    held, mixed = lax.optimization_barrier((held, mixed))
    pieces = [mixed] + [shift(mixed, "lon", s) for s in range(1, shards)]
    held = stash(field, weights, 1 + first, second, total, first, held)
    held, edges, halo = lax.optimization_barrier((held, edges, halo))
    return block(
        index, field, halo, held, weights, jnp.asarray(inverse), edges, conv_bias[None, :], pieces
    )


def solution(mesh):
    in_specs = (P("lat", "lon", None), P("lon", None, None, None), P(), P())
    out_specs = P("lat", "lon", None)
    return jax.shard_map(
        per_device, mesh=mesh, in_specs=in_specs, out_specs=out_specs, check_vma=False
    )
```

```python
import functools
import math

import jax
import jax.numpy as jnp
import ml_dtypes
import numpy as np
from jax import lax
from jax.experimental import pallas as pl
from jax.experimental.pallas import tpu as pltpu
from jax.sharding import PartitionSpec as P

M = 64
NLON = 3600
TILE = 512
LAG = 16
VMEM = 56 * 1024 * 1024


def tables(shards, lon_dev, modes_local):
    angle = np.arange(NLON, dtype=np.float32) * np.float32(2.0 * math.pi / NLON)
    cos, sin = np.cos(angle), np.sin(angle)
    forward, inverse = [], []
    for index in range(shards):
        places = np.arange(lon_dev) + index * lon_dev

        def rows(step):
            owners = [(index + step * s) % shards for s in range(shards)]
            modes = np.concatenate([np.arange(modes_local) + o * modes_local for o in owners])
            return modes, modes[:, None] * places[None, :] % NLON

        modes, phase = rows(1)
        scale = np.float32(1.0 / math.sqrt(NLON))
        table = np.stack([cos[phase] * scale, -sin[phase] * scale], axis=1)
        forward.append(table.reshape(2 * len(modes), lon_dev))
        modes, phase = rows(-1)
        weight = (np.where(modes == 0, 1.0, 2.0) / math.sqrt(4.0 * M)).astype(np.float32)[:, None]
        table = np.stack([weight * cos[phase], -weight * sin[phase]], axis=1)
        inverse.append(table.reshape(2 * len(modes), lon_dev).T)
    return (
        np.stack(forward).astype(ml_dtypes.bfloat16),
        np.stack(inverse).astype(ml_dtypes.bfloat16),
    )


def dft_kernel(mine, index_ref, table_ref, *refs):
    x_refs, (own_ref, send_ref) = refs[:-2], refs[-2:]
    channels = own_ref.shape[2]
    for n, x_ref in enumerate(x_refs):
        l = 2 * n
        pair = jnp.concatenate([x_ref[0], x_ref[1]], axis=1)
        part = jnp.dot(table_ref[...], pair, preferred_element_type=jnp.float32)
        for d in range(2):
            half = part[:, d * channels : (d + 1) * channels]
            own_ref[l + d] = half[:mine]
            send_ref[l + d] = half[mine:].astype(jnp.bfloat16)


def forward_dft(index, field, table, mine):
    lat, lon, channels = field.shape
    streams = 4
    rows = 2 * streams
    count = table.shape[1]
    return pl.pallas_call(
        functools.partial(dft_kernel, mine),
        grid_spec=pltpu.PrefetchScalarGridSpec(
            num_scalar_prefetch=1,
            grid=(lat // rows,),
            in_specs=[
                pl.BlockSpec((None, count, lon), lambda i, index: (index[0], 0, 0)),
            ]
            + [
                pl.BlockSpec(
                    (2, lon, channels), functools.partial(lambda n, i, index: (streams * i + n, 0, 0), n)
                )
                for n in range(streams)
            ],
            out_specs=[
                pl.BlockSpec((rows, mine, channels), lambda i, index: (i, 0, 0)),
                pl.BlockSpec((rows, count - mine, channels), lambda i, index: (i, 0, 0)),
            ],
        ),
        out_shape=[
            jax.ShapeDtypeStruct((lat, mine, channels), jnp.float32),
            jax.ShapeDtypeStruct((lat, count - mine, channels), jnp.bfloat16),
        ],
        compiler_params=pltpu.CompilerParams(vmem_limit_bytes=VMEM),
        cost_estimate=pl.CostEstimate(
            flops=2 * count * lat * lon * channels,
            bytes_accessed=2 * lat * lon * channels + 6 * lat * count * channels,
            transcendentals=0,
        ),
        name="forward_dft",
    )(index, table, *[field] * streams)


def mix_kernel(parts, own_ref, *refs):
    recv_refs, (w_ref, out_ref, s_ref, t_ref) = refs[:parts], refs[parts:]
    lat, mine, channels = own_ref.shape
    step = pl.program_id(0)
    group = w_ref.shape[0]

    @pl.when(step == 0)
    def _():
        total = own_ref[...]
        for recv_ref in recv_refs:
            total = total + recv_ref[...].astype(jnp.float32)
        s_ref[...] = total.reshape(lat * mine, channels)

    for g in range(group):
        m = step * group + g
        real = pl.ds(2 * m, lat, stride=mine)
        imag = pl.ds(2 * m + 1, lat, stride=mine)
        joined = jnp.concatenate(
            [s_ref[real, :].astype(jnp.bfloat16), s_ref[imag, :].astype(jnp.bfloat16)], axis=1
        )
        upper = jnp.concatenate([w_ref[g, 0], w_ref[g, 1]], axis=1)
        lower = jnp.concatenate([-w_ref[g, 1], w_ref[g, 0]], axis=1)
        block = jnp.concatenate([upper, lower], axis=0)
        product = jnp.dot(joined, block, preferred_element_type=jnp.float32)
        t_ref[real, :] = product[:, :channels]
        t_ref[imag, :] = product[:, channels:]

    @pl.when(step == pl.num_programs(0) - 1)
    def _():
        out_ref[...] = t_ref[...].reshape(lat, mine, channels).astype(jnp.bfloat16)


def mix_modes(own, received, spectral_weight):
    lat, mine, channels = own.shape
    modes = spectral_weight.shape[0]
    group = math.gcd(modes, 8)
    whole = pl.BlockSpec((lat, mine, channels), lambda i: (0, 0, 0))
    return pl.pallas_call(
        functools.partial(mix_kernel, len(received)),
        grid=(modes // group,),
        in_specs=[whole] * (1 + len(received))
        + [pl.BlockSpec((group, 2, channels, channels), lambda i: (i, 0, 0, 0))],
        out_specs=whole,
        out_shape=jax.ShapeDtypeStruct((lat, mine, channels), jnp.bfloat16),
        scratch_shapes=[pltpu.VMEM((lat * mine, channels), jnp.float32)] * 2,
        compiler_params=pltpu.CompilerParams(vmem_limit_bytes=VMEM),
        cost_estimate=pl.CostEstimate(
            flops=8 * modes * lat * channels * channels,
            bytes_accessed=4 * modes * channels * channels + 8 * lat * mine * channels,
            transcendentals=0,
        ),
        name="mix_modes",
    )(own, *received, spectral_weight)


def cuts(length):
    starts = list(range(0, max(length - TILE // 2, 1), TILE))
    return list(zip(starts, starts[1:] + [length]))


def convolve(a_ref, rows_ref, here, w_ref, low, high, channels, extra=None):
    lhs = jnp.concatenate([rows_ref[slot, low:high] for slot in here], axis=1)
    for j in range(3):
        result = jnp.dot(lhs, w_ref[j], preferred_element_type=jnp.float32)
        if j == 1 and extra is not None:
            result = result + jnp.dot(*extra, preferred_element_type=jnp.float32)
        for d in range(2):
            a_ref[j, d, 8 + low : 8 + high] = result[:, d * channels : (d + 1) * channels]


def taps(a_ref, d, low, size):
    return (
        a_ref[0, d, pl.ds(7 + low, size)]
        + a_ref[1, d, pl.ds(8 + low, size)]
        + a_ref[2, d, pl.ds(9 + low, size)]
    )


def stash_kernel(first, count, x_ref, w_ref, *refs):
    out_ref, rows_ref, a_ref, sems = refs[-4:]
    lon, channels = x_ref.shape[1:]
    step = pl.program_id(0)
    pair = first + step
    slots = rows_ref.shape[0]

    def fetch(place):
        slot = lax.rem(place, slots)
        return pltpu.make_async_copy(x_ref.at[place - 1], rows_ref.at[slot], sems.at[slot])

    @pl.when(step == 0)
    def _():
        for i in range(4):
            fetch(2 * pair + i).start()
        for i in range(2):
            fetch(2 * pair + i).wait()

    @pl.when(step + 1 < count)
    def _():
        for i in range(4, 6):
            fetch(2 * pair + i).start()

    for i in range(2, 4):
        fetch(2 * pair + i).wait()

    here = [lax.rem(2 * pair + i, slots) for i in range(4)]
    for d in range(2):
        a_ref[0, d, 7:8] = jnp.zeros((1, channels), jnp.float32)
        a_ref[2, d, 8 + lon : 9 + lon] = jnp.zeros((1, channels), jnp.float32)

    def finish(low, high):
        for d in range(2):
            out_ref[d, low:high] = taps(a_ref, d, low, high - low).astype(jnp.bfloat16)

    done, ready = 0, 0
    for low, high in cuts(lon):
        convolve(a_ref, rows_ref, here, w_ref, low, high, channels)
        if ready > done:
            finish(done, ready)
            done = ready
        ready = high - LAG
    finish(done, lon)


def stash(field, weights, first, count, total, offset, before=None):
    lat, lon, channels = field.shape
    slots = 8
    extra = [] if before is None else [before]
    return pl.pallas_call(
        functools.partial(stash_kernel, first, count),
        grid=(count,),
        in_specs=[
            pl.BlockSpec(memory_space=pl.ANY),
            pl.BlockSpec(weights.shape, lambda i: (0, 0, 0)),
        ]
        + [pl.BlockSpec(memory_space=pl.ANY)] * len(extra),
        out_specs=pl.BlockSpec((2, lon, channels), lambda i: (i + offset, 0, 0)),
        out_shape=jax.ShapeDtypeStruct((2 * total, lon, channels), jnp.bfloat16),
        input_output_aliases={2: 0} if extra else {},
        scratch_shapes=[
            pltpu.VMEM((slots, lon, channels), jnp.bfloat16),
            pltpu.VMEM((3, 2, (lon + 8) // 8 * 8 + 16, channels), jnp.float32),
            pltpu.SemaphoreType.DMA((slots,)),
        ],
        compiler_params=pltpu.CompilerParams(vmem_limit_bytes=VMEM),
        cost_estimate=pl.CostEstimate(
            flops=2 * 2 * count * lon * channels * 12 * channels,
            bytes_accessed=8 * count * lon * channels,
            transcendentals=0,
        ),
        name="stash",
    )(field, weights, *extra)


def block_kernel(
    stashed, pieces, index_ref, x_ref, halo_ref, stash_ref, w_ref, g_ref, edge_ref, bias_ref, *refs
):
    piece_refs, (out_ref, rows_ref, rhs_ref, a_ref, sems) = refs[:pieces], refs[pieces:]
    lat, lon, channels = x_ref.shape
    step = pl.program_id(0)
    slots = rows_ref.shape[0]
    last = lat // 2 - 1
    base = 1 + stashed
    wrap = lat + 2

    def virtual(at):
        return jnp.where(at == last, last + 2, at + 1)

    def fetch(source, place):
        slot = lax.rem(place, slots)
        return pltpu.make_async_copy(source, rows_ref.at[slot], sems.at[slot])

    def start(place):
        real = jnp.where(place >= wrap, place - wrap, place)

        @pl.when(real == 0)
        def _():
            fetch(halo_ref.at[0], place).start()

        @pl.when(real == lat + 1)
        def _():
            fetch(halo_ref.at[1], place).start()

        @pl.when(jnp.logical_and(real > 0, real < lat + 1))
        def _():
            fetch(x_ref.at[jnp.clip(real - 1, 0, lat - 1)], place).start()

    def wait(place):
        fetch(halo_ref.at[0], place).wait()

    def fresh(pair):
        return jnp.logical_or(pair == base, pair == last + 2)

    def begin(at):
        pair = virtual(at)

        @pl.when(fresh(pair))
        def _():
            start(2 * pair)
            start(2 * pair + 1)

        @pl.when(pair >= base)
        def _():
            start(2 * pair + 2)
            start(2 * pair + 3)

    if stashed == 0:
        @pl.when(step == 0)
        def _():
            begin(step)

    @pl.when(step < last)
    def _():
        begin(step + 1)

    top = 0
    for piece_ref in piece_refs:
        size = piece_ref.shape[1]
        for d in range(2):
            rhs_ref[top : top + size, d * channels : (d + 1) * channels] = piece_ref[d]
        top += size
    bias = bias_ref[...]
    c1 = math.sqrt(2.0 / math.pi)
    c2 = c1 * 0.044715

    def gelu(x):
        t = jnp.tanh(x * (c1 + c2 * (x * x)))
        return (x * (0.5 + 0.5 * t)).astype(jnp.bfloat16)

    pair = virtual(step)

    @pl.when(pair < base)
    def _():
        for low, high in cuts(lon):
            part = jnp.dot(g_ref[low:high], rhs_ref[...], preferred_element_type=jnp.float32)
            for d in range(2):
                x = part[:, d * channels : (d + 1) * channels] + stash_ref[d, low:high].astype(jnp.float32)
                x = x + bias
                place = low + lax.broadcasted_iota(jnp.int32, x.shape, 0)
                if low == 0:
                    x = x + jnp.where(place == 0, edge_ref[d, 0:1], 0.0)
                if high == lon:
                    x = x + jnp.where(place == lon - 1, edge_ref[d, 1:2], 0.0)
                out_ref[d, low:high] = gelu(x)

    @pl.when(pair >= base)
    def _():
        @pl.when(fresh(pair))
        def _():
            wait(2 * pair)
            wait(2 * pair + 1)

        wait(2 * pair + 2)
        wait(2 * pair + 3)
        here = [lax.rem(2 * pair + i, slots) for i in range(4)]
        for d in range(2):
            a_ref[0, d, 7:8] = edge_ref[d, 0:1]
            a_ref[2, d, 8 + lon : 9 + lon] = edge_ref[d, 1:2]

        def finish(low, high):
            for d in range(2):
                out_ref[d, low:high] = gelu(taps(a_ref, d, low, high - low) + bias)

        done, ready = 0, 0
        for low, high in cuts(lon):
            extra = (g_ref[low:high], rhs_ref[...])
            convolve(a_ref, rows_ref, here, w_ref, low, high, channels, extra)
            if ready > done:
                finish(done, ready)
                done = ready
            ready = high - LAG
        finish(done, lon)


def block(index, field, halo, stashed, weights, table, edges, bias, pieces):
    lat, lon, channels = field.shape
    count = table.shape[2]
    slots = 8
    pairs = lat // 2
    held = stashed.shape[0] // 2

    def pair(i, index):
        return (lax.rem(i + 1, pairs), 0, 0)

    return pl.pallas_call(
        functools.partial(block_kernel, held, len(pieces)),
        grid_spec=pltpu.PrefetchScalarGridSpec(
            num_scalar_prefetch=1,
            grid=(pairs,),
            in_specs=[
                pl.BlockSpec(memory_space=pl.ANY),
                pl.BlockSpec(memory_space=pl.ANY),
                pl.BlockSpec(
                    (2, lon, channels), lambda i, index: (jnp.minimum(i, held - 1), 0, 0)
                ),
                pl.BlockSpec(weights.shape, lambda i, index: (0, 0, 0)),
                pl.BlockSpec((None, lon, count), lambda i, index: (index[0], 0, 0)),
                pl.BlockSpec((2, 2, channels), pair),
                pl.BlockSpec((1, channels), lambda i, index: (0, 0)),
            ]
            + [pl.BlockSpec((2, p.shape[1], channels), pair) for p in pieces],
            out_specs=pl.BlockSpec((2, lon, channels), pair),
            scratch_shapes=[
                pltpu.VMEM((slots, lon, channels), jnp.bfloat16),
                pltpu.VMEM((count, 2 * channels), jnp.bfloat16),
                pltpu.VMEM((3, 2, (lon + 8) // 8 * 8 + 16, channels), jnp.float32),
                pltpu.SemaphoreType.DMA((slots,)),
            ],
        ),
        out_shape=jax.ShapeDtypeStruct((lat, lon, channels), jnp.bfloat16),
        compiler_params=pltpu.CompilerParams(vmem_limit_bytes=VMEM),
        cost_estimate=pl.CostEstimate(
            flops=2 * lat * lon * channels * (9 * channels + count),
            bytes_accessed=4 * lat * lon * channels,
            transcendentals=lat * lon * channels,
        ),
        name="block",
    )(index, field, halo, stashed, weights, table, edges, bias, *pieces)


def shift(x, axis, by, periodic=True):
    count = lax.axis_size(axis)
    pairs = [(i, (i + by) % count) for i in range(count) if periodic or 0 <= i + by < count]
    return lax.ppermute(x, axis, pairs)


def pair_weights(conv_weight):
    zero = jnp.zeros_like(conv_weight[0, 0])
    return jnp.stack(
        [
            jnp.concatenate(
                [
                    jnp.concatenate([conv_weight[i, j] if i < 3 else zero for i in range(4)], axis=0),
                    jnp.concatenate([conv_weight[i - 1, j] if i else zero for i in range(4)], axis=0),
                ],
                axis=1,
            )
            for j in range(3)
        ]
    )


def per_device(field, spectral_weight, conv_weight, conv_bias):
    lat, lon, channels = field.shape
    modes_local = spectral_weight.shape[0]
    shards = lax.axis_size("lon")
    index = lax.axis_index("lon")
    mine = 2 * modes_local
    forward, inverse = tables(shards, lon, modes_local)
    index = index.astype(jnp.int32)[None]
    weights = pair_weights(conv_weight)

    own, send = forward_dft(index, field, jnp.asarray(forward), mine)
    received = [shift(send[:, (s - 1) * mine : s * mine], "lon", s) for s in range(1, shards)]

    outer = (field[lat - 1 :], field[:1], field[:, lon - 1], field[:, 0], weights)
    outer, send = lax.optimization_barrier((outer, send))
    low_row, high_row, east_column, west_column, weights = outer
    above = shift(low_row, "lat", 1, False)
    below = shift(high_row, "lat", -1, False)
    easts = jnp.concatenate([above[:, lon - 1], east_column, below[:, lon - 1]], axis=0)
    wests = jnp.concatenate([above[:, 0], west_column, below[:, 0]], axis=0)
    if shards == 2:
        columns = shift(jnp.stack([easts, wests], axis=1), "lon", 1)
    else:
        columns = jnp.stack([shift(easts, "lon", 1), shift(wests, "lon", -1)], axis=1)
    edges = jnp.stack(
        [
            sum(
                jnp.dot(
                    columns[i : i + lat, side],
                    conv_weight[i, 2 * side],
                    preferred_element_type=jnp.float32,
                )
                for i in range(3)
            )
            for side in range(2)
        ],
        axis=1,
    )
    halo = jnp.concatenate([above, below], axis=0)

    first, second = lat // 12, 7 * lat // 48
    total = first + second
    held = stash(field, weights, 1, first, total, 0)
    held, received = lax.optimization_barrier((held, received))
    mixed = mix_modes(own, received, spectral_weight)
    held, mixed = lax.optimization_barrier((held, mixed))
    pieces = [mixed] + [shift(mixed, "lon", s) for s in range(1, shards)]
    held = stash(field, weights, 1 + first, second, total, first, held)
    held, edges, halo = lax.optimization_barrier((held, edges, halo))
    return block(
        index, field, halo, held, weights, jnp.asarray(inverse), edges, conv_bias[None, :], pieces
    )


def solution(mesh):
    in_specs = (P("lat", "lon", None), P("lon", None, None, None), P(), P())
    out_specs = P("lat", "lon", None)
    return jax.shard_map(
        per_device, mesh=mesh, in_specs=in_specs, out_specs=out_specs, check_vma=False
    )
```
